32 devices in a mesh: dp: 4 (over y, x), ctx: 2 (over core), tp: 4 (over z).
Axes of the slice: x: 2, y: 2, z: 4, core: 2. Of those that a mesh axis runs over, the one named last changes fastest.
Arguments:
- block_input: bfloat16 [2048, 1024], P(('dp', 'ctx')), may hold values from -6 to 6
- qkv_weight: bfloat16 [1024, 3, 1024], P('dp', None, 'tp'), may hold values from -0.125 to 0.125
- qv_bias: bfloat16 [2, 16, 64], P(None, 'tp', 'dp'), may hold values from -3 to 3
- proj_weight: bfloat16 [1024, 1024], P('dp', 'tp'), may hold values from -0.75 to 0.75
- fc_weight: bfloat16 [1024, 4096], P('dp', 'tp'), may hold values from -0.1875 to 0.1875
- fc_bias: bfloat16 [32, 128], P('tp', 'dp'), may hold values from -3 to 3
- out_weight: bfloat16 [1024, 4096], P('dp', 'tp'), may hold values from -0.09375 to 0.09375
- norm_gains: bfloat16 [2, 1024], P(None, 'dp'), may hold values from 0.5 to 1.5
- shifts: bfloat16 [4, 1024], P(None, 'dp'), may hold values from -2 to 2
- segment_ids: int32 [4, 512], P('dp'), may hold values from 0 to 3, as said below
- out_grad: bfloat16 [2048, 1024], P(('dp', 'ctx')), may hold values from -6 to 6
Outputs:
- block_output: float32 [2048, 1024], P(('dp', 'ctx'))
- input_grad: float32 [2048, 1024], P(('dp', 'ctx'))
- qkv_weight_grad: float32 [1024, 3, 1024], P('dp', None, 'tp')
- qv_bias_grad: float32 [2, 16, 64], P(None, 'tp', 'dp')
- proj_weight_grad: float32 [1024, 1024], P('dp', 'tp')
- fc_weight_grad: float32 [1024, 4096], P('dp', 'tp')
- fc_bias_grad: float32 [32, 128], P('tp', 'dp')
- out_weight_grad: float32 [1024, 4096], P('dp', 'tp')
- norm_gains_grad: float32 [2, 1024], P(None, 'dp')
- shifts_grad: float32 [4, 1024], P(None, 'dp')
The draws below stay inside these ranges and needn't reach their ends.
Inputs may be any that keep to these rules, and one draw needn't show every extreme that they name: `segment_ids`: within each sequence the document numbers never fall and all 4 appear; each document covers 64 to 256 positions, one exactly 256 and one exactly 64.
All inputs are finite; a program needn't handle non-finite values.
Results may differ from the reference program's by a relative error of at most 0.012.
Values may be sent and summed in bfloat16 or wider, within the bound.
A program may use at most 128 MiB of HBM per device.

```python
import jax
import jax.numpy as jnp
from jax import lax

D = 1024
HEADS = 16
HEAD_DIM = 64
FF = 4096
SEQ_LEN = 512
ROW_W = 128
SEQS = 4
TOKENS = 2048
N_TP = 4


def draw_block_input(key, part):
    main_key = jax.random.fold_in(key, 1)
    return jax.random.truncated_normal(main_key, -6.0, 6.0, (TOKENS, D), jnp.float32).astype(jnp.bfloat16)


def draw_qkv_weight(key, part):
    main_key = jax.random.fold_in(key, 2)
    weight_scale = D ** (-0.5)
    return (jax.random.truncated_normal(main_key, -4.0, 4.0, (D, 3, D), jnp.float32) * weight_scale).astype(jnp.bfloat16)


def draw_segment_ids(key, part):
    fewest = SEQ_LEN // 8

    def one_row(row_key):
        size_key, order_key = jax.random.split(row_key)
        middle = jax.random.randint(size_key, (), fewest, SEQ_LEN // 4 + 1).astype(jnp.int32)
        doc_sizes = jnp.stack([jnp.full((), SEQ_LEN // 2, jnp.int32), jnp.full((), fewest, jnp.int32), middle, (3 * SEQ_LEN // 8 - middle).astype(jnp.int32)])
        doc_sizes = doc_sizes[jax.random.permutation(order_key, 4)]
        doc_ends = jnp.cumsum(doc_sizes).astype(jnp.int32)
        positions = jnp.arange(SEQ_LEN, dtype=jnp.int32)
        return jnp.sum((positions[:, None] >= doc_ends[None, :3]).astype(jnp.int32), axis=1)
    return jax.vmap(one_row)(jax.random.split(jax.random.fold_in(key, 3), SEQS))


def levels(key, extent, shards, smallest, largest):
    gain, own = 1.0, jax.random.fold_in(key, 6)
    for position, shards_of in shards:
        draws = jnp.exp(jax.random.uniform(jax.random.fold_in(own, position), (shards_of,), jnp.float32, smallest / len(shards), largest / len(shards)))
        gain = gain * jnp.repeat(draws, extent[position] // shards_of).reshape([-1 if axis == position else 1 for axis in range(len(extent))])
    return gain


def gaussian(rng, extent, spread, reach, cuts=(), held_as=jnp.bfloat16):
    result = jax.random.normal(rng, extent, jnp.float32) * spread
    if len(cuts) > 0:
        result = levels(rng, extent, cuts, -0.22, 0.18) * result
    return jnp.clip(result, min=-reach, max=reach).astype(held_as)


def setup_inputs(seed: int = 0) -> dict:
    key_list = jax.random.split(jax.random.key(seed), 12)
    block_input = draw_block_input(jax.random.fold_in(key_list[11], 71), 0)
    qkv_weight = draw_qkv_weight(jax.random.fold_in(key_list[11], 71), 0)
    qv_bias = gaussian(key_list[2], (2, HEADS, HEAD_DIM), 0.5, 3.0, ((1, 4), (2, 4)))
    proj_weight = gaussian(key_list[3], (D, D), (D // 16) ** -0.5, 0.75, ((0, 4), (1, 4)))
    fc_weight = gaussian(key_list[4], (D, FF), D ** -0.5, 0.1875, ((0, 4), (1, 4)))
    fc_bias = gaussian(key_list[5], (FF // ROW_W, ROW_W), 0.5, 3.0, ((0, 4), (1, 4)))
    out_weight = gaussian(key_list[6], (D, FF), FF ** -0.5, 0.09375, ((0, 4), (1, 4)))
    norm_gains = jnp.clip(1.0 + 0.1 * jax.random.normal(key_list[7], (2, D), jnp.float32), 0.5, 1.5).astype(jnp.bfloat16)
    shifts = gaussian(key_list[8], (4, D), 0.3, 2.0, ((1, 4),))
    segment_ids = draw_segment_ids(jax.random.fold_in(key_list[11], 71), 0)
    out_grad = gaussian(key_list[10], (TOKENS, D), 1.0, 6.0, ((0, 8),))
    return dict(block_input=block_input, qkv_weight=qkv_weight, qv_bias=qv_bias, proj_weight=proj_weight, fc_weight=fc_weight, fc_bias=fc_bias, out_weight=out_weight, norm_gains=norm_gains, shifts=shifts, segment_ids=segment_ids, out_grad=out_grad)


EPSILON = 1e-05
MASKED_SCORE = -1e+30
GELU_SCALE = 0.7978845608028654

def layer_norm(values, gain_row, shift_row):
    centered = values - lax.optimization_barrier(jnp.mean(values, axis=-1, keepdims=True))
    inverse = lax.rsqrt(lax.optimization_barrier(jnp.mean(centered * centered, axis=-1, keepdims=True)) + EPSILON)
    normed = centered * inverse
    return (normed, inverse, normed * gain_row + shift_row)

def norm_back(upstream, normed, inverse, gain_row):
    scaled = upstream * gain_row
    return inverse * (scaled - lax.optimization_barrier(jnp.mean(scaled, axis=-1, keepdims=True)) - normed * lax.optimization_barrier(jnp.mean(scaled * normed, axis=-1, keepdims=True)))

def gelu_slope(pre_act):
    inner_arg = GELU_SCALE * (pre_act + 0.044715 * pre_act * pre_act * pre_act)
    tanh_val = jnp.tanh(inner_arg)
    activated = 0.5 * pre_act * (1.0 + tanh_val)
    slopes = 0.5 * (1.0 + tanh_val) + 0.5 * pre_act * (1.0 - tanh_val * tanh_val) * GELU_SCALE * (1.0 + 3.0 * 0.044715 * pre_act * pre_act)
    return (activated, slopes)

def summed_groups(group_terms):
    return group_terms.sum(axis=0)

def reference(block_input, qkv_weight, qv_bias, proj_weight, fc_weight, fc_bias, out_weight, norm_gains, shifts, segment_ids, out_grad):
    gains_f = norm_gains.astype(jnp.float32)
    shifts_f = shifts.astype(jnp.float32)
    bias_qv = qv_bias.astype(jnp.float32).reshape(2, D)
    bias_fc = fc_bias.astype(jnp.float32).reshape(FF)
    group_width = D // N_TP
    group_hidden = FF // N_TP
    proj_groups = proj_weight.astype(jnp.float32).reshape(D, N_TP, group_width)
    fc_groups = fc_weight.astype(jnp.float32).reshape(D, N_TP, group_hidden)
    out_groups = out_weight.astype(jnp.float32).reshape(D, N_TP, group_hidden)
    qkv_groups = qkv_weight.astype(jnp.float32).reshape(D, 3, N_TP, group_width)
    qkv_flat = qkv_weight.reshape(D, 3 * D)
    score_scale = HEAD_DIM ** (-0.5)
    positions = jnp.arange(SEQ_LEN, dtype=jnp.int32)

    def one_sequence(totals, pieces):
        seq_input, seq_grad, seq_ids = pieces
        input_f32 = seq_input.astype(jnp.float32)
        normed1, inverse1, ln1_float = layer_norm(input_f32, gains_f[0], shifts_f[0])
        ln1_out = ln1_float.astype(jnp.bfloat16)
        packed = jnp.dot(ln1_out, qkv_flat, preferred_element_type=jnp.float32).reshape(SEQ_LEN, 3, D)
        queries = (packed[:, 0] + bias_qv[0]).astype(jnp.bfloat16)
        keys_all = packed[:, 1].astype(jnp.bfloat16)
        values_all = (packed[:, 2] + bias_qv[1]).astype(jnp.bfloat16)
        query_heads = queries.astype(jnp.float32).reshape(SEQ_LEN, HEADS, HEAD_DIM)
        key_heads = keys_all.astype(jnp.float32).reshape(SEQ_LEN, HEADS, HEAD_DIM)
        value_heads = values_all.astype(jnp.float32).reshape(SEQ_LEN, HEADS, HEAD_DIM)
        live_mask = (seq_ids[:, None] == seq_ids[None, :]) & (positions[None, :] <= positions[:, None])
        raw_scores = jnp.einsum('qhd,khd->hqk', query_heads, key_heads) * score_scale
        scores = jnp.where(live_mask[None], raw_scores, MASKED_SCORE)
        row_max = lax.optimization_barrier(jnp.max(scores, axis=-1, keepdims=True))
        log_total = row_max + jnp.log(lax.optimization_barrier(jnp.sum(jnp.exp(scores - row_max), axis=-1, keepdims=True)))
        probs_f = jnp.exp(scores - log_total)
        probs_b = probs_f.astype(jnp.bfloat16)
        attn_out = jnp.einsum('hqk,khd->qhd', probs_b.astype(jnp.float32), value_heads).astype(jnp.bfloat16).reshape(SEQ_LEN, D)
        head_terms = jnp.einsum('lgc,dgc->gld', attn_out.astype(jnp.float32).reshape(SEQ_LEN, N_TP, group_width), proj_groups)
        resid = input_f32 + summed_groups(head_terms) + shifts_f[2]
        normed2, inverse2, ln2_float = layer_norm(resid, gains_f[1], shifts_f[1])
        ln2_out = ln2_float.astype(jnp.bfloat16)
        pre_act = jnp.dot(ln2_out, fc_weight, preferred_element_type=jnp.float32) + bias_fc
        activated, slopes = gelu_slope(pre_act)
        act_b = activated.astype(jnp.bfloat16)
        mlp_terms = jnp.einsum('lgf,dgf->gld', act_b.astype(jnp.float32).reshape(SEQ_LEN, N_TP, group_hidden), out_groups)
        output = resid + summed_groups(mlp_terms) + shifts_f[3]
        grad_f32 = seq_grad.astype(jnp.float32)
        out_w_grad = jnp.dot(seq_grad.T, act_b, preferred_element_type=jnp.float32)
        out_b_grad = lax.optimization_barrier(jnp.sum(grad_f32, axis=0))
        hidden_grad = (jnp.dot(seq_grad, out_weight, preferred_element_type=jnp.float32) * slopes).astype(jnp.bfloat16)
        fc_b_grad = lax.optimization_barrier(jnp.sum(hidden_grad.astype(jnp.float32), axis=0))
        fc_w_grad = jnp.dot(ln2_out.T, hidden_grad, preferred_element_type=jnp.float32)
        norm2_grad = summed_groups(jnp.einsum('lgf,dgf->gld', hidden_grad.astype(jnp.float32).reshape(SEQ_LEN, N_TP, group_hidden), fc_groups))
        gain2_grad = lax.optimization_barrier(jnp.sum(norm2_grad * normed2, axis=0))
        shift2_grad = lax.optimization_barrier(jnp.sum(norm2_grad, axis=0))
        resid_grad = grad_f32 + norm_back(norm2_grad, normed2, inverse2, gains_f[1])
        proj_b_grad = lax.optimization_barrier(jnp.sum(resid_grad, axis=0))
        resid_grad_b = resid_grad.astype(jnp.bfloat16)
        proj_w_grad = jnp.dot(resid_grad_b.T, attn_out, preferred_element_type=jnp.float32)
        attn_grad = jnp.dot(resid_grad_b, proj_weight, preferred_element_type=jnp.float32).astype(jnp.bfloat16)
        attn_grad_h = attn_grad.astype(jnp.float32).reshape(SEQ_LEN, HEADS, HEAD_DIM)
        attn_out_h = attn_out.astype(jnp.float32).reshape(SEQ_LEN, HEADS, HEAD_DIM)
        prob_grad = jnp.einsum('qhd,khd->hqk', attn_grad_h, value_heads)
        row_delta = jnp.transpose(lax.optimization_barrier(jnp.sum(attn_grad_h * attn_out_h, axis=-1)))[:, :, None]
        score_grad = (probs_f * (prob_grad - row_delta) * score_scale).astype(jnp.bfloat16).astype(jnp.float32)
        query_grad = jnp.einsum('hqk,khd->qhd', score_grad, key_heads).astype(jnp.bfloat16).reshape(SEQ_LEN, D)
        key_grad = jnp.einsum('hqk,qhd->khd', score_grad, query_heads).astype(jnp.bfloat16).reshape(SEQ_LEN, D)
        value_grad = jnp.einsum('hqk,qhd->khd', probs_b.astype(jnp.float32), attn_grad_h).astype(jnp.bfloat16).reshape(SEQ_LEN, D)
        qv_b_grad = jnp.stack([lax.optimization_barrier(jnp.sum(query_grad.astype(jnp.float32), axis=0)), lax.optimization_barrier(jnp.sum(value_grad.astype(jnp.float32), axis=0))])
        stacked = jnp.stack([query_grad, key_grad, value_grad], axis=1)
        qkv_w_grad = jnp.dot(ln1_out.T, stacked.reshape(SEQ_LEN, 3 * D), preferred_element_type=jnp.float32).reshape(D, 3, D)
        norm1_grad = summed_groups(jnp.einsum('ltgc,dtgc->gld', stacked.astype(jnp.float32).reshape(SEQ_LEN, 3, N_TP, group_width), qkv_groups))
        gain1_grad = lax.optimization_barrier(jnp.sum(norm1_grad * normed1, axis=0))
        shift1_grad = lax.optimization_barrier(jnp.sum(norm1_grad, axis=0))
        input_grad = resid_grad + norm_back(norm1_grad, normed1, inverse1, gains_f[0])
        updates = (qkv_w_grad, qv_b_grad, proj_w_grad, fc_w_grad, fc_b_grad, out_w_grad, jnp.stack([gain1_grad, gain2_grad]), jnp.stack([shift1_grad, shift2_grad, proj_b_grad, out_b_grad]))
        new_totals = tuple((total + update for total, update in zip(totals, updates)))
        return (new_totals, (output, input_grad))
    zero_totals = (jnp.zeros((D, 3, D), jnp.float32), jnp.zeros((2, D), jnp.float32), jnp.zeros((D, D), jnp.float32), jnp.zeros((D, FF), jnp.float32), jnp.zeros((FF,), jnp.float32), jnp.zeros((D, FF), jnp.float32), jnp.zeros((2, D), jnp.float32), jnp.zeros((4, D), jnp.float32))
    totals, (outputs, input_grads) = lax.scan(one_sequence, zero_totals, (block_input.reshape(SEQS, SEQ_LEN, D), out_grad.reshape(SEQS, SEQ_LEN, D), segment_ids))
    return (outputs.reshape(TOKENS, D), input_grads.reshape(TOKENS, D), totals[0], totals[1].reshape(2, HEADS, HEAD_DIM), totals[2], totals[3], totals[4].reshape(FF // ROW_W, ROW_W), totals[5], totals[6], totals[7])
```

```python
import functools

import jax
import jax.numpy as jnp
from jax import lax
from jax.experimental import pallas as pl
from jax.experimental.pallas import tpu as pltpu
from jax.sharding import PartitionSpec as P

EPSILON = 1e-05
MASKED_SCORE = -1e30
GELU_SCALE = 0.7978845608028654
F32, BF16 = jnp.float32, jnp.bfloat16
MESH = pl.DeviceIdType.MESH
TILE = 256


def normalize(values):
    centered = values - jnp.mean(values, axis=-1, keepdims=True)
    inverse = lax.rsqrt(jnp.mean(centered * centered, axis=-1, keepdims=True) + EPSILON)
    return centered * inverse, inverse


def norm_back(upstream, normed, inverse, gain_row):
    scaled = upstream * gain_row
    return inverse * (
        scaled
        - jnp.mean(scaled, axis=-1, keepdims=True)
        - normed * jnp.mean(scaled * normed, axis=-1, keepdims=True)
    )


def gelu_slope(pre_act):
    inner_arg = GELU_SCALE * (pre_act + 0.044715 * pre_act * pre_act * pre_act)
    tanh_val = jnp.tanh(inner_arg)
    activated = 0.5 * pre_act * (1.0 + tanh_val)
    slopes = 0.5 * (1.0 + tanh_val) + 0.5 * pre_act * (1.0 - tanh_val * tanh_val) * GELU_SCALE * (
        1.0 + 3.0 * 0.044715 * pre_act * pre_act
    )
    return (activated, slopes)


def dot_nn(a, b):
    return lax.dot_general(a, b, (((1,), (0,)), ((), ())), preferred_element_type=F32)


def dot_nt(a, b):
    return lax.dot_general(a, b, (((1,), (1,)), ((), ())), preferred_element_type=F32)


def dot_tn(a, b):
    return lax.dot_general(a, b, (((0,), (0,)), ((), ())), preferred_element_type=F32)


def loop(count, body):
    def step(j, carry):
        body(j)
        return carry

    lax.fori_loop(0, count, step, 0)


def tile_at(j, size=TILE):
    return pl.ds(pl.multiple_of(j * size, size), size)


def layer_kernel(
    nd, nt, head_dim,
    x_ref, gy_ref, small_ref, mask_ref, lq_ref, lp_ref, lf_ref, lo_ref,
    out_ref, ing_ref, gq_ref, gp_ref, gf_ref, go_ref, gs_ref,
    wq, wp, wf, wo, small_in, small_f, ln1_s, q_s, kv_s, prob_s, attn_s,
    part, rs_in, ag, resid_s, dact_s, act_s, dpre_s, dresid_s, dkv_own, dkv_out, dkv_in, st_s,
    loc_q, loc_p, loc_f, loc_o, par_q, par_p, par_f, par_o,
    sum_q, sum_p, sum_f, sum_o, rcv_q, rcv_p, rcv_f, rcv_o,
    tp_small, own_small, ctx_small, dp_small, send_sems, recv_sems,
):
    d, c, t = lax.axis_index("dp"), lax.axis_index("ctx"), lax.axis_index("tp")
    other = 1 - c
    rows, width = x_ref.shape
    local = q_s.shape[1]
    hidden = act_s.shape[1]
    heads = local // head_dim
    block = lq_ref.shape[0]
    half = block // 2
    own_rows = rows // nt
    scale = head_dim ** (-0.5)
    count = [0]
    pending = []

    def send(src, dst, **where):
        i = count[0]
        count[0] += 1
        copy = pltpu.make_async_remote_copy(
            src_ref=src, dst_ref=dst, send_sem=send_sems.at[i], recv_sem=recv_sems.at[i],
            device_id=where, device_id_type=MESH,
        )
        copy.start()
        pending.append(copy)
        return copy

    def dp_at(k):
        return lax.rem(d + k, nd)

    def tp_at(k):
        return lax.rem(t + k, nt)

    def mine(size=own_rows):
        return pl.ds(pl.multiple_of(t * size, size), size)

    barrier = pltpu.get_barrier_semaphore()
    for k in range(1, nd):
        pl.semaphore_signal(barrier, inc=1, device_id={"dp": dp_at(k)}, device_id_type=MESH)
    for k in range(1, nt):
        pl.semaphore_signal(barrier, inc=1, device_id={"tp": tp_at(k)}, device_id_type=MESH)
    pl.semaphore_signal(barrier, inc=1, device_id={"ctx": other}, device_id_type=MESH)
    pl.semaphore_wait(barrier, nd + nt - 1)

    small_copies = [send(small_ref, small_in.at[d], dp=dp_at(k)) for k in range(1, nd)]

    def half_at(owner, core):
        return pl.ds(pl.multiple_of(owner * block + core * half, half), half)

    def gather(shard, whole):
        return [
            send(shard.at[pl.ds(pl.multiple_of(c * half, half), half)], whole.at[half_at(d, c)],
                 dp=dp_at(k))
            for k in range(1, nd)
        ]

    def hand_on(whole, copies):
        handed = []
        for k in range(1, nd):
            copies[k - 1].wait_recv()
            place = whole.at[half_at(lax.rem(d - k + nd, nd), c)]
            handed.append(send(place, place, ctx=other))
        return handed

    def arrive(copies):
        for copy in copies:
            copy.wait_recv()

    got_q = gather(lq_ref, wq)
    got_p = gather(lp_ref, wp)
    got_f = gather(lf_ref, wf)
    got_o = gather(lo_ref, wo)
    own_block = pl.ds(pl.multiple_of(d * block, block), block)
    for shard, whole in ((lq_ref, wq), (lp_ref, wp), (lf_ref, wf), (lo_ref, wo)):
        whole[own_block, :] = shard[...]
    small_in[d] = small_ref[...]

    arrive(small_copies)
    total = small_in[0].astype(F32)
    for k in range(1, nd):
        total = total + small_in[k].astype(F32)
    small_f[...] = total

    def first_norm(j):
        at = tile_at(j, own_rows)
        normed, _ = normalize(x_ref[at, :].astype(F32))
        ln1_s[at, :] = (normed * small_f[0:1, :] + small_f[2:3, :]).astype(BF16)

    loop(nt, first_norm)
    handed = hand_on(wq, got_q)
    arrive(handed)
    kv_s[0:rows, 0:local] = dot_nn(ln1_s[...], wq[:, local : 2 * local]).astype(BF16)
    kv_s[0:rows, local : 2 * local] = (
        dot_nn(ln1_s[...], wq[:, 2 * local : 3 * local]) + small_f[7:8, local : 2 * local]
    ).astype(BF16)
    kv_copy = send(kv_s.at[pl.ds(0, rows)], kv_s.at[pl.ds(rows, rows)], ctx=other)
    q_s[...] = (dot_nn(ln1_s[...], wq[:, 0:local]) + small_f[7:8, 0:local]).astype(BF16)
    handed_p = hand_on(wp, got_p)
    kv_copy.wait_recv()

    mixed = []
    for h in range(heads):
        at = slice(h * head_dim, (h + 1) * head_dim)
        vat = slice(local + h * head_dim, local + (h + 1) * head_dim)
        scores = dot_nt(q_s[:, at], kv_s[:, at]) * scale + mask_ref[...].astype(F32)
        top = jnp.max(scores, axis=-1, keepdims=True)
        log_total = top + jnp.log(jnp.sum(jnp.exp(scores - top), axis=-1, keepdims=True))
        probs = jnp.exp(scores - log_total)
        prob_s[h] = probs
        mixed.append(dot_nn(probs.astype(BF16), kv_s[:, vat]))
    attn_s[...] = jnp.concatenate(mixed, axis=1).astype(BF16)

    def reduce_start(i):
        return [
            send(part.at[i, pl.ds(pl.multiple_of(tp_at(k) * own_rows, own_rows), own_rows)],
                 rs_in.at[i, k - 1], tp=tp_at(k))
            for k in range(1, nt)
        ]

    def reduce_end(i, copies):
        total = part[i, mine(), :].astype(F32)
        for k in range(1, nt):
            copies[k - 1].wait_recv()
            total = total + rs_in[i, k - 1].astype(F32)
        return total

    def share(i, value):
        ag[i, mine(), :] = value.astype(BF16)
        place = ag.at[i, mine()]
        return [send(place, place, tp=tp_at(k)) for k in range(1, nt)]

    arrive(handed_p)

    def proj_tile(j):
        part[0, :, tile_at(j)] = dot_nt(attn_s[...], wp[tile_at(j), :]).astype(BF16)

    loop(width // TILE, proj_tile)
    reduced = reduce_start(0)
    handed_f = hand_on(wf, got_f)
    own_x = x_ref[mine(), :].astype(F32)
    resid = own_x + reduce_end(0, reduced) + small_f[4:5, :]
    resid_s[...] = resid
    normed2, _ = normalize(resid)
    shared = share(0, normed2 * small_f[1:2, :] + small_f[3:4, :])
    handed_o = hand_on(wo, got_o)
    arrive(handed_f)
    arrive(handed_o)

    def dact_tile(j):
        dact_s[:, tile_at(j)] = dot_nn(gy_ref[...], wo[:, tile_at(j)])

    loop(hidden // TILE, dact_tile)
    arrive(shared)

    def hidden_tile(j):
        at = tile_at(j)
        pre = dot_nn(ag[0], wf[:, at]) + small_f[6:7, at]
        activated, slopes = gelu_slope(pre)
        act_s[:, at] = activated.astype(BF16)
        dpre = (dact_s[:, at] * slopes).astype(BF16)
        dpre_s[:, at] = dpre
        own_small[6:7, at] = jnp.sum(dpre.astype(F32), axis=0, keepdims=True)

    loop(hidden // TILE, hidden_tile)

    def dln2_tile(j):
        part[1, :, tile_at(j)] = dot_nt(dpre_s[...], wf[tile_at(j), :]).astype(BF16)

    loop(width // TILE, dln2_tile)
    reduced1 = reduce_start(1)

    def down_tile(j):
        part[2, :, tile_at(j)] = dot_nt(act_s[...], wo[tile_at(j), :]).astype(BF16)

    loop(width // TILE, down_tile)
    reduced2 = reduce_start(2)

    tile_rows = max(TILE, block)
    blocks_in = tile_rows // block

    def grad_start(left, right, grads, partner):
        def tile(j):
            value = dot_tn(left[:, tile_at(j, tile_rows)], right[...]).astype(BF16)
            grads[pl.ds(j * blocks_in, blocks_in)] = value.reshape(
                (blocks_in, 2, half, value.shape[1])
            )

        loop(width // tile_rows, tile)
        return send(grads.at[:, other], partner, ctx=other)

    def grad_spread(copy, grads, partner, sums, received):
        copy.wait_recv()

        def add(j):
            sums[j] = (grads[j, c].astype(F32) + partner[j].astype(F32)).astype(BF16)

        loop(nd, add)
        return [send(sums.at[dp_at(k)], received.at[k - 1], dp=dp_at(k)) for k in range(1, nd)]

    def grad_end(copies, sums, received, result):
        total = sums[d].astype(F32)
        for k in range(1, nd):
            copies[k - 1].wait_recv()
            total = total + received[k - 1].astype(F32)
        place = pl.ds(pl.multiple_of(c * half, half), half)
        result[place, :] = total
        return send(result.at[place], result.at[place], ctx=other)

    pair_o = grad_start(gy_ref, act_s, loc_o, par_o)

    dln2 = reduce_end(1, reduced1)
    normed2, inverse2 = normalize(resid_s[...])
    own_gy = gy_ref[mine(), :].astype(F32)
    dresid = own_gy + norm_back(dln2, normed2, inverse2, small_f[1:2, :])
    shared1 = share(1, dresid)
    dresid_s[...] = dresid
    tp_small[t, 1:2, :] = jnp.sum(dln2 * normed2, axis=0, keepdims=True)
    tp_small[t, 3:4, :] = jnp.sum(dln2, axis=0, keepdims=True)
    tp_small[t, 4:5, :] = jnp.sum(dresid, axis=0, keepdims=True)
    tp_small[t, 5:6, :] = jnp.sum(own_gy, axis=0, keepdims=True)
    spread_o = grad_spread(pair_o, loc_o, par_o, sum_o, rcv_o)
    pair_f = grad_start(ag.at[0], dpre_s, loc_f, par_f)
    arrive(shared1)
    shared2 = share(2, resid_s[...] + reduce_end(2, reduced2) + small_f[5:6, :])

    dattn = dot_nn(ag[1], wp[...]).astype(BF16)
    dq_parts, dk_parts, dv_parts = [], [], []
    for h in range(heads):
        at = slice(h * head_dim, (h + 1) * head_dim)
        vat = slice(local + h * head_dim, local + (h + 1) * head_dim)
        dattn_h = dattn[:, at]
        probs = prob_s[h]
        delta = jnp.sum(
            dattn_h.astype(F32) * attn_s[:, at].astype(F32), axis=-1, keepdims=True
        )
        dprob = dot_nt(dattn_h, kv_s[:, vat])
        dscore = (probs * (dprob - delta) * scale).astype(BF16)
        dq_parts.append(dot_nn(dscore, kv_s[:, at]))
        dk_parts.append(dot_tn(dscore, q_s[:, at]))
        dv_parts.append(dot_tn(probs.astype(BF16), dattn_h))
    dkv = jnp.concatenate(dk_parts + dv_parts, axis=1)
    dkv_out[...] = dkv[rows:, :]
    dkv_copy = send(dkv_out, dkv_in, ctx=other)
    dkv_own[...] = dkv[:rows, :]
    dq = jnp.concatenate(dq_parts, axis=1).astype(BF16)
    st_s[:, 0:local] = dq
    spread_f = grad_spread(pair_f, loc_f, par_f, sum_f, rcv_f)
    dkv_copy.wait_recv()
    st_s[:, local : 3 * local] = (dkv_own[...] + dkv_in[...]).astype(BF16)

    def dln1_tile(j):
        part[3, :, tile_at(j)] = dot_nt(st_s[...], wq[tile_at(j), :]).astype(BF16)

    loop(width // TILE, dln1_tile)
    reduced3 = reduce_start(3)
    pair_q = grad_start(ln1_s, st_s, loc_q, par_q)
    pair_p = grad_start(ag.at[1], attn_s, loc_p, par_p)
    own_small[7:8, :] = jnp.zeros((1, width), F32)
    own_small[7:8, 0:local] = jnp.sum(st_s[:, 0:local].astype(F32), axis=0, keepdims=True)
    own_small[7:8, local : 2 * local] = jnp.sum(
        st_s[:, 2 * local : 3 * local].astype(F32), axis=0, keepdims=True
    )
    spread_q = grad_spread(pair_q, loc_q, par_q, sum_q, rcv_q)
    spread_p = grad_spread(pair_p, loc_p, par_p, sum_p, rcv_p)

    dln1 = reduce_end(3, reduced3)
    normed1, inverse1 = normalize(x_ref[mine(), :].astype(F32))
    shared3 = share(3, dresid_s[...] + norm_back(dln1, normed1, inverse1, small_f[0:1, :]))
    tp_small[t, 0:1, :] = jnp.sum(dln1 * normed1, axis=0, keepdims=True)
    tp_small[t, 2:3, :] = jnp.sum(dln1, axis=0, keepdims=True)
    tp_small[t, 6:8, :] = jnp.zeros((2, width), F32)
    small_tp = [send(tp_small.at[t], tp_small.at[t], tp=tp_at(k)) for k in range(1, nt)]
    end_o = grad_end(spread_o, sum_o, rcv_o, go_ref)
    end_f = grad_end(spread_f, sum_f, rcv_f, gf_ref)
    arrive(small_tp)
    total = tp_small[0]
    for k in range(1, nt):
        total = total + tp_small[k]
    ctx_small[c, 0:6, :] = total[0:6]
    ctx_small[c, 6:8, :] = own_small[6:8, :]
    small_ctx = send(ctx_small.at[c], ctx_small.at[c], ctx=other)
    arrive(shared2)
    out_ref[...] = ag[2].astype(F32)
    small_ctx.wait_recv()
    dp_small[d] = ctx_small[0] + ctx_small[1]
    small_dp = [send(dp_small.at[d], dp_small.at[d], dp=dp_at(k)) for k in range(1, nd)]
    end_q = grad_end(spread_q, sum_q, rcv_q, gq_ref)
    end_p = grad_end(spread_p, sum_p, rcv_p, gp_ref)
    arrive(small_dp)
    total = dp_small[0]
    for k in range(1, nd):
        total = total + dp_small[k]
    gs_ref[...] = total
    arrive(shared3)
    ing_ref[...] = ag[3].astype(F32)
    arrive([end_o, end_f, end_q, end_p])
    for copy in pending:
        copy.wait_send()


def per_device(
    nd, nt,
    block_input, qkv_weight, qv_bias, proj_weight, fc_weight, fc_bias, out_weight,
    norm_gains, shifts, segment_ids, out_grad,
):
    d, c = lax.axis_index("dp"), lax.axis_index("ctx")
    rows, width = block_input.shape
    block, _, local = qkv_weight.shape
    hidden = fc_weight.shape[1]
    heads_here, head_part = qv_bias.shape[1:]
    head_dim = head_part * nd
    table_rows, table_part = fc_bias.shape
    seq_len = segment_ids.shape[1]
    half = block // 2
    own_rows = rows // nt

    def widen(shard, axis):
        shape = list(shard.shape)
        size = shape[axis]
        shape[axis] = size * nd
        start = [0] * len(shape)
        start[axis] = d * size
        return lax.dynamic_update_slice(jnp.zeros(shape, shard.dtype), shard, start)

    rows_of = [
        widen(norm_gains, 1),
        widen(shifts, 1),
        widen(fc_bias, 1).reshape(1, hidden),
        jnp.pad(widen(qv_bias, 2).reshape(1, 2 * local), ((0, 0), (0, width - 2 * local))),
        jnp.zeros((8, width), BF16),
    ]
    small = jnp.concatenate(rows_of, axis=0)

    seg = segment_ids[0]
    pos = jnp.arange(rows, dtype=jnp.int32)
    q_pos = c * rows + pos
    k_pos = jnp.concatenate([q_pos, (1 - c) * rows + pos])
    seg_q = lax.dynamic_slice_in_dim(seg, c * rows, rows)
    seg_k = jnp.concatenate([seg_q, lax.dynamic_slice_in_dim(seg, (1 - c) * rows, rows)])
    live = (seg_q[:, None] == seg_k[None, :]) & (k_pos[None, :] <= q_pos[:, None])
    mask = jnp.where(live, 0.0, MASKED_SCORE).astype(BF16)

    widths = (3 * local, local, hidden, hidden)
    vmem = pltpu.VMEM
    scratch = (
        [vmem((width, w), BF16) for w in widths]
        + [
            vmem((nd, 16, width), BF16),
            vmem((16, width), F32),
            vmem((rows, width), BF16),
            vmem((rows, local), BF16),
            vmem((2 * rows, 2 * local), BF16),
            vmem((heads_here, rows, 2 * rows), F32),
            vmem((rows, local), BF16),
            vmem((4, rows, width), BF16),
            vmem((4, nt - 1, own_rows, width), BF16),
            vmem((4, rows, width), BF16),
            vmem((own_rows, width), F32),
            vmem((rows, hidden), F32),
            vmem((rows, hidden), BF16),
            vmem((rows, hidden), BF16),
            vmem((own_rows, width), F32),
            vmem((rows, 2 * local), F32),
            vmem((rows, 2 * local), F32),
            vmem((rows, 2 * local), F32),
            vmem((rows, 3 * local), BF16),
        ]
        + [vmem((nd, 2, half, w), BF16) for w in widths]
        + [vmem((nd, half, w), BF16) for w in widths]
        + [vmem((nd, half, w), BF16) for w in widths]
        + [vmem((nd - 1, half, w), BF16) for w in widths]
        + [
            vmem((nt, 8, width), F32),
            vmem((8, width), F32),
            vmem((2, 8, width), F32),
            vmem((nd, 8, width), F32),
            pltpu.SemaphoreType.DMA((14 * (nd - 1) + 10 * (nt - 1) + 16,)),
            pltpu.SemaphoreType.DMA((14 * (nd - 1) + 10 * (nt - 1) + 16,)),
        ]
    )
    whole = pl.BlockSpec(memory_space=pltpu.VMEM)
    out_shapes = [
        (rows, width), (rows, width), (block, 3 * local), (block, local),
        (block, hidden), (block, hidden), (8, width),
    ]
    output, input_grad, g_qkv, g_proj, g_fc, g_out, g_small = pl.pallas_call(
        functools.partial(layer_kernel, nd, nt, head_dim),
        out_shape=[jax.ShapeDtypeStruct(shape, F32) for shape in out_shapes],
        in_specs=[whole] * 8,
        out_specs=[whole] * 7,
        scratch_shapes=scratch,
        compiler_params=pltpu.CompilerParams(
            collective_id=0, has_side_effects=True, vmem_limit_bytes=60 * 1024 * 1024
        ),
    )(
        block_input, out_grad, small, mask, qkv_weight.reshape(block, 3 * local),
        proj_weight, fc_weight, out_weight,
    )

    part_of = functools.partial(lax.dynamic_slice_in_dim, g_small, d * block, block, 1)()
    g_gains, g_shifts = part_of[0:2], part_of[2:6]
    g_fc_bias = lax.dynamic_slice_in_dim(
        g_small[6].reshape(table_rows, table_part * nd), d * table_part, table_part, 1
    )
    g_qv = lax.dynamic_slice_in_dim(
        g_small[7, : 2 * local].reshape(2, heads_here, head_dim), d * head_part, head_part, 2
    )
    return (
        output, input_grad, g_qkv.reshape(block, 3, local), g_qv, g_proj, g_fc, g_fc_bias,
        g_out, g_gains, g_shifts,
    )


def solution(mesh):
    in_specs = (
        P(("dp", "ctx"), None),
        P("dp", None, "tp"),
        P(None, "tp", "dp"),
        P("dp", "tp"),
        P("dp", "tp"),
        P("tp", "dp"),
        P("dp", "tp"),
        P(None, "dp"),
        P(None, "dp"),
        P("dp", None),
        P(("dp", "ctx"), None),
    )
    out_specs = (
        P(("dp", "ctx"), None),
        P(("dp", "ctx"), None),
        P("dp", None, "tp"),
        P(None, "tp", "dp"),
        P("dp", "tp"),
        P("dp", "tp"),
        P("tp", "dp"),
        P("dp", "tp"),
        P(None, "dp"),
        P(None, "dp"),
    )
    return jax.shard_map(
        functools.partial(per_device, mesh.shape["dp"], mesh.shape["tp"]),
        mesh=mesh, in_specs=in_specs, out_specs=out_specs, check_vma=False,
    )
```

```python
import functools

import jax
import jax.numpy as jnp
from jax import lax
from jax.experimental import pallas as pl
from jax.experimental.pallas import tpu as pltpu
from jax.sharding import PartitionSpec as P

EPSILON = 1e-05
MASKED_SCORE = -1e30
GELU_SCALE = 0.7978845608028654
F32, BF16 = jnp.float32, jnp.bfloat16
MESH = pl.DeviceIdType.MESH
TILE = 256


def normalize(values):
    centered = values - jnp.mean(values, axis=-1, keepdims=True)
    inverse = lax.rsqrt(jnp.mean(centered * centered, axis=-1, keepdims=True) + EPSILON)
    return centered * inverse, inverse


def norm_back(upstream, normed, inverse, gain_row):
    scaled = upstream * gain_row
    return inverse * (
        scaled
        - jnp.mean(scaled, axis=-1, keepdims=True)
        - normed * jnp.mean(scaled * normed, axis=-1, keepdims=True)
    )


def gelu_slope(pre_act):
    inner_arg = GELU_SCALE * (pre_act + 0.044715 * pre_act * pre_act * pre_act)
    tanh_val = jnp.tanh(inner_arg)
    activated = 0.5 * pre_act * (1.0 + tanh_val)
    slopes = 0.5 * (1.0 + tanh_val) + 0.5 * pre_act * (1.0 - tanh_val * tanh_val) * GELU_SCALE * (
        1.0 + 3.0 * 0.044715 * pre_act * pre_act
    )
    return (activated, slopes)


def dot_nn(a, b):
    return lax.dot_general(a, b, (((1,), (0,)), ((), ())), preferred_element_type=F32)


def dot_nt(a, b):
    return lax.dot_general(a, b, (((1,), (1,)), ((), ())), preferred_element_type=F32)


def dot_tn(a, b):
    return lax.dot_general(a, b, (((0,), (0,)), ((), ())), preferred_element_type=F32)


def loop(count, body):
    def step(j, carry):
        body(j)
        return carry

    lax.fori_loop(0, count, step, 0)


def tile_at(j, size=TILE):
    return pl.ds(pl.multiple_of(j * size, size), size)


def layer_kernel(
    nd, nt, head_dim,
    x_ref, gy_ref, gains_ref, shifts_ref, fcb_ref, qvb_ref, seg_ref, lq_ref, lp_ref, lf_ref, lo_ref,
    out_ref, ing_ref, gq_ref, gp_ref, gf_ref, go_ref, ggains_ref, gshifts_ref, gfcb_ref, gqvb_ref,
    wq, wp, wf, wo, small_in, small_f, mask_ref, ln1_s, q_s, kv_s, prob_s, attn_s,
    part, rs_in, ag, resid_s, dact_s, act_s, dpre_s, dresid_s, dkv_own, dkv_out, dkv_in, st_s,
    loc_q, loc_p, loc_f, loc_o, par_q, par_p, par_f, par_o,
    sum_q, sum_p, sum_f, sum_o, rcv_q, rcv_p, rcv_f, rcv_o,
    tp_small, own_small, ctx_small, dp_small, send_sems, recv_sems,
):
    d, c, t = lax.axis_index("dp"), lax.axis_index("ctx"), lax.axis_index("tp")
    other = 1 - c
    rows, width = x_ref.shape
    local = q_s.shape[1]
    hidden = act_s.shape[1]
    heads = local // head_dim
    block = lq_ref.shape[0]
    half = block // 2
    own_rows = rows // nt
    scale = head_dim ** (-0.5)
    count = [0]
    pending = []

    def send(src, dst, **where):
        i = count[0]
        count[0] += 1
        copy = pltpu.make_async_remote_copy(
            src_ref=src, dst_ref=dst, send_sem=send_sems.at[i], recv_sem=recv_sems.at[i],
            device_id=where, device_id_type=MESH,
        )
        copy.start()
        pending.append(copy)
        return copy

    def dp_at(k):
        return lax.rem(d + k, nd)

    def tp_at(k):
        return lax.rem(t + k, nt)

    def mine(size=own_rows):
        return pl.ds(pl.multiple_of(t * size, size), size)

    barrier = pltpu.get_barrier_semaphore()
    for k in range(1, nd):
        pl.semaphore_signal(barrier, inc=1, device_id={"dp": dp_at(k)}, device_id_type=MESH)
    for k in range(1, nt):
        pl.semaphore_signal(barrier, inc=1, device_id={"tp": tp_at(k)}, device_id_type=MESH)
    pl.semaphore_signal(barrier, inc=1, device_id={"ctx": other}, device_id_type=MESH)
    pl.semaphore_wait(barrier, nd + nt - 1)

    def place(shard):
        size = shard.shape[1]
        lanes = lax.broadcasted_iota(jnp.int32, (shard.shape[0], size * nd), 1)
        spread = jnp.concatenate([shard.astype(F32)] * nd, axis=1)
        return jnp.where((lanes >= d * size) & (lanes < (d + 1) * size), spread, 0.0)

    def in_a_row(tables):
        return jnp.concatenate([tab[r : r + 1] for tab in tables for r in range(tab.shape[0])], axis=1)


    def half_at(owner, core):
        return pl.ds(pl.multiple_of(owner * block + core * half, half), half)

    def gather(shard, whole):
        return [
            send(shard.at[pl.ds(pl.multiple_of(c * half, half), half)], whole.at[half_at(d, c)],
                 dp=dp_at(k))
            for k in range(1, nd)
        ]

    def hand_on(whole, copies):
        handed = []
        for k in range(1, nd):
            copies[k - 1].wait_recv()
            place = whole.at[half_at(lax.rem(d - k + nd, nd), c)]
            handed.append(send(place, place, ctx=other))
        return handed

    def arrive(copies):
        for copy in copies:
            copy.wait_recv()

    got_q = gather(lq_ref, wq)
    got_p = gather(lp_ref, wp)
    got_f = gather(lf_ref, wf)
    got_o = gather(lo_ref, wo)
    small_in[d, 0:2, :] = place(gains_ref[...])
    small_in[d, 2:6, :] = place(shifts_ref[...])
    small_in[d, 6:7, :] = in_a_row([place(fcb_ref[...])])
    small_in[d, 7:8, :] = jnp.zeros((1, width), F32)
    small_in[d, 7:8, 0 : 2 * local] = in_a_row([place(qvb_ref[m]) for m in range(2)])
    small_copies = [send(small_in.at[d], small_in.at[d], dp=dp_at(k)) for k in range(1, nd)]
    seg_own = seg_ref[:, pl.ds(pl.multiple_of(c * rows, rows), rows)].astype(F32)
    seg_rest = seg_ref[:, pl.ds(pl.multiple_of(other * rows, rows), rows)].astype(F32)
    seg_column = jnp.transpose(jnp.broadcast_to(seg_own, (128, rows)))[:, 0:1]
    seg_keys = jnp.concatenate([seg_own, seg_rest], axis=1)
    q_pos = c * rows + lax.broadcasted_iota(jnp.int32, (rows, 2 * rows), 0)
    lane = lax.broadcasted_iota(jnp.int32, (rows, 2 * rows), 1)
    k_pos = lane + jnp.where(lane < rows, c * rows, other * rows - rows)
    mask_ref[...] = jnp.where((seg_column == seg_keys) & (k_pos <= q_pos), 0.0, MASKED_SCORE)
    own_block = pl.ds(pl.multiple_of(d * block, block), block)
    for shard, whole in ((lq_ref, wq), (lp_ref, wp), (lf_ref, wf), (lo_ref, wo)):
        whole[own_block, :] = shard[...]
    arrive(small_copies)
    total = small_in[0]
    for k in range(1, nd):
        total = total + small_in[k]
    small_f[...] = total

    def first_norm(j):
        at = tile_at(j, own_rows)
        normed, _ = normalize(x_ref[at, :].astype(F32))
        ln1_s[at, :] = (normed * small_f[0:1, :] + small_f[2:3, :]).astype(BF16)

    loop(nt, first_norm)
    handed = hand_on(wq, got_q)
    arrive(handed)
    kv_s[0:rows, 0:local] = dot_nn(ln1_s[...], wq[:, local : 2 * local]).astype(BF16)
    kv_s[0:rows, local : 2 * local] = (
        dot_nn(ln1_s[...], wq[:, 2 * local : 3 * local]) + small_f[7:8, local : 2 * local]
    ).astype(BF16)
    kv_copy = send(kv_s.at[pl.ds(0, rows)], kv_s.at[pl.ds(rows, rows)], ctx=other)
    q_s[...] = (dot_nn(ln1_s[...], wq[:, 0:local]) + small_f[7:8, 0:local]).astype(BF16)
    handed_p = hand_on(wp, got_p)
    kv_copy.wait_recv()

    mixed = []
    for h in range(heads):
        at = slice(h * head_dim, (h + 1) * head_dim)
        vat = slice(local + h * head_dim, local + (h + 1) * head_dim)
        scores = dot_nt(q_s[:, at], kv_s[:, at]) * scale + mask_ref[...]
        top = jnp.max(scores, axis=-1, keepdims=True)
        log_total = top + jnp.log(jnp.sum(jnp.exp(scores - top), axis=-1, keepdims=True))
        probs = jnp.exp(scores - log_total)
        prob_s[h] = probs
        mixed.append(dot_nn(probs.astype(BF16), kv_s[:, vat]))
    attn_s[...] = jnp.concatenate(mixed, axis=1).astype(BF16)

    def reduce_start(i):
        return [
            send(part.at[i, pl.ds(pl.multiple_of(tp_at(k) * own_rows, own_rows), own_rows)],
                 rs_in.at[i, k - 1], tp=tp_at(k))
            for k in range(1, nt)
        ]

    def reduce_end(i, copies):
        total = part[i, mine(), :].astype(F32)
        for k in range(1, nt):
            copies[k - 1].wait_recv()
            total = total + rs_in[i, k - 1].astype(F32)
        return total

    def share(i, value):
        ag[i, mine(), :] = value.astype(BF16)
        place = ag.at[i, mine()]
        return [send(place, place, tp=tp_at(k)) for k in range(1, nt)]

    arrive(handed_p)

    def proj_tile(j):
        part[0, :, tile_at(j)] = dot_nt(attn_s[...], wp[tile_at(j), :]).astype(BF16)

    loop(width // TILE, proj_tile)
    reduced = reduce_start(0)
    handed_f = hand_on(wf, got_f)
    own_x = x_ref[mine(), :].astype(F32)
    resid = own_x + reduce_end(0, reduced) + small_f[4:5, :]
    resid_s[...] = resid
    normed2, _ = normalize(resid)
    shared = share(0, normed2 * small_f[1:2, :] + small_f[3:4, :])
    handed_o = hand_on(wo, got_o)
    arrive(handed_f)
    arrive(handed_o)

    def dact_tile(j):
        dact_s[:, tile_at(j)] = dot_nn(gy_ref[...], wo[:, tile_at(j)])

    loop(hidden // TILE, dact_tile)
    arrive(shared)

    def hidden_tile(j):
        at = tile_at(j)
        pre = dot_nn(ag[0], wf[:, at]) + small_f[6:7, at]
        activated, slopes = gelu_slope(pre)
        act_s[:, at] = activated.astype(BF16)
        dpre = (dact_s[:, at] * slopes).astype(BF16)
        dpre_s[:, at] = dpre
        own_small[6:7, at] = jnp.sum(dpre.astype(F32), axis=0, keepdims=True)

    loop(hidden // TILE, hidden_tile)

    def dln2_tile(j):
        part[1, :, tile_at(j)] = dot_nt(dpre_s[...], wf[tile_at(j), :]).astype(BF16)

    loop(width // TILE, dln2_tile)
    reduced1 = reduce_start(1)

    def down_tile(j):
        part[2, :, tile_at(j)] = dot_nt(act_s[...], wo[tile_at(j), :]).astype(BF16)

    loop(width // TILE, down_tile)

    tile_rows = max(TILE, block)
    blocks_in = tile_rows // block

    def grad_start(left, right, grads, partner):
        def tile(j):
            value = dot_tn(left[:, tile_at(j, tile_rows)], right[...]).astype(BF16)
            grads[pl.ds(j * blocks_in, blocks_in)] = value.reshape(
                (blocks_in, 2, half, value.shape[1])
            )

        loop(width // tile_rows, tile)
        return send(grads.at[:, other], partner, ctx=other)

    def grad_spread(copy, grads, partner, sums, received):
        copy.wait_recv()

        def add(j):
            sums[j] = (grads[j, c].astype(F32) + partner[j].astype(F32)).astype(BF16)

        loop(nd, add)
        return [send(sums.at[dp_at(k)], received.at[k - 1], dp=dp_at(k)) for k in range(1, nd)]

    def grad_end(copies, sums, received, result):
        total = sums[d].astype(F32)
        for k in range(1, nd):
            copies[k - 1].wait_recv()
            total = total + received[k - 1].astype(F32)
        place = pl.ds(pl.multiple_of(c * half, half), half)
        result[place, :] = total
        return send(result.at[place], result.at[place], ctx=other)

    pair_o = grad_start(gy_ref, act_s, loc_o, par_o)

    dln2 = reduce_end(1, reduced1)
    normed2, inverse2 = normalize(resid_s[...])
    own_gy = gy_ref[mine(), :].astype(F32)
    dresid = own_gy + norm_back(dln2, normed2, inverse2, small_f[1:2, :])
    shared1 = share(1, dresid)
    reduced2 = reduce_start(2)
    dresid_s[...] = dresid
    tp_small[t, 1:2, :] = jnp.sum(dln2 * normed2, axis=0, keepdims=True)
    tp_small[t, 3:4, :] = jnp.sum(dln2, axis=0, keepdims=True)
    tp_small[t, 4:5, :] = jnp.sum(dresid, axis=0, keepdims=True)
    tp_small[t, 5:6, :] = jnp.sum(own_gy, axis=0, keepdims=True)
    spread_o = grad_spread(pair_o, loc_o, par_o, sum_o, rcv_o)
    pair_f = grad_start(ag.at[0], dpre_s, loc_f, par_f)
    arrive(shared1)

    dattn = dot_nn(ag[1], wp[...]).astype(BF16)
    dq_parts, dk_parts, dv_parts = [], [], []
    for h in range(heads):
        at = slice(h * head_dim, (h + 1) * head_dim)
        vat = slice(local + h * head_dim, local + (h + 1) * head_dim)
        dattn_h = dattn[:, at]
        probs = prob_s[h]
        delta = jnp.sum(
            dattn_h.astype(F32) * attn_s[:, at].astype(F32), axis=-1, keepdims=True
        )
        dprob = dot_nt(dattn_h, kv_s[:, vat])
        dscore = (probs * (dprob - delta) * scale).astype(BF16)
        dq_parts.append(dot_nn(dscore, kv_s[:, at]))
        dk_parts.append(dot_tn(dscore, q_s[:, at]))
        dv_parts.append(dot_tn(probs.astype(BF16), dattn_h))
    dkv = jnp.concatenate(dk_parts + dv_parts, axis=1)
    dkv_out[...] = dkv[rows:, :]
    dkv_copy = send(dkv_out, dkv_in, ctx=other)
    dkv_own[...] = dkv[:rows, :]
    dq = jnp.concatenate(dq_parts, axis=1).astype(BF16)
    st_s[:, 0:local] = dq
    spread_f = grad_spread(pair_f, loc_f, par_f, sum_f, rcv_f)
    dkv_copy.wait_recv()
    st_s[:, local : 3 * local] = (dkv_own[...] + dkv_in[...]).astype(BF16)

    def dln1_tile(j):
        part[3, :, tile_at(j)] = dot_nt(st_s[...], wq[tile_at(j), :]).astype(BF16)

    loop(width // TILE, dln1_tile)
    reduced3 = reduce_start(3)
    pair_q = grad_start(ln1_s, st_s, loc_q, par_q)
    pair_p = grad_start(ag.at[1], attn_s, loc_p, par_p)
    own_small[7:8, :] = jnp.zeros((1, width), F32)
    own_small[7:8, 0:local] = jnp.sum(st_s[:, 0:local].astype(F32), axis=0, keepdims=True)
    own_small[7:8, local : 2 * local] = jnp.sum(
        st_s[:, 2 * local : 3 * local].astype(F32), axis=0, keepdims=True
    )
    spread_q = grad_spread(pair_q, loc_q, par_q, sum_q, rcv_q)
    spread_p = grad_spread(pair_p, loc_p, par_p, sum_p, rcv_p)

    shared2 = share(2, resid_s[...] + reduce_end(2, reduced2) + small_f[5:6, :])
    dln1 = reduce_end(3, reduced3)
    normed1, inverse1 = normalize(x_ref[mine(), :].astype(F32))
    shared3 = share(3, dresid_s[...] + norm_back(dln1, normed1, inverse1, small_f[0:1, :]))
    tp_small[t, 0:1, :] = jnp.sum(dln1 * normed1, axis=0, keepdims=True)
    tp_small[t, 2:3, :] = jnp.sum(dln1, axis=0, keepdims=True)
    tp_small[t, 6:8, :] = jnp.zeros((2, width), F32)
    small_tp = [send(tp_small.at[t], tp_small.at[t], tp=tp_at(k)) for k in range(1, nt)]
    end_o = grad_end(spread_o, sum_o, rcv_o, go_ref)
    end_f = grad_end(spread_f, sum_f, rcv_f, gf_ref)
    arrive(small_tp)
    total = tp_small[0]
    for k in range(1, nt):
        total = total + tp_small[k]
    ctx_small[c, 0:6, :] = total[0:6]
    ctx_small[c, 6:8, :] = own_small[6:8, :]
    small_ctx = send(ctx_small.at[c], ctx_small.at[c], ctx=other)
    arrive(shared2)
    out_ref[...] = ag[2].astype(F32)
    small_ctx.wait_recv()
    dp_small[d] = ctx_small[0] + ctx_small[1]
    small_dp = [send(dp_small.at[d], dp_small.at[d], dp=dp_at(k)) for k in range(1, nd)]
    end_q = grad_end(spread_q, sum_q, rcv_q, gq_ref)
    end_p = grad_end(spread_p, sum_p, rcv_p, gp_ref)
    arrive(small_dp)
    total = dp_small[0]
    for k in range(1, nd):
        total = total + dp_small[k]

    def own_part(table):
        size = table.shape[1] // nd
        part_here = jnp.zeros((table.shape[0], size), F32)
        for k in range(nd):
            part_here = jnp.where(d == k, table[:, k * size : (k + 1) * size], part_here)
        return part_here

    def as_table(row, columns, count):
        return jnp.concatenate(
            [row[:, r * columns : (r + 1) * columns] for r in range(count)], axis=0
        )

    ggains_ref[...] = own_part(total[0:2])
    gshifts_ref[...] = own_part(total[2:6])
    table_rows = fcb_ref.shape[0]
    gfcb_ref[...] = own_part(as_table(total[6:7], hidden // table_rows, table_rows))
    for m in range(2):
        gqvb_ref[m] = own_part(as_table(total[7:8, m * local : (m + 1) * local], head_dim, heads))
    arrive(shared3)
    ing_ref[...] = ag[3].astype(F32)
    arrive([end_o, end_f, end_q, end_p])
    for copy in pending:
        copy.wait_send()


def move_kernel(count, *refs):
    sems = refs[2 * count]
    copies = [pltpu.make_async_copy(refs[i], refs[count + i], sems.at[i]) for i in range(count)]
    for copy in copies:
        copy.start()
    for copy in copies:
        copy.wait()


def per_device(
    nd, nt,
    block_input, qkv_weight, qv_bias, proj_weight, fc_weight, fc_bias, out_weight,
    norm_gains, shifts, segment_ids, out_grad,
):
    rows, width = block_input.shape
    block, _, local = qkv_weight.shape
    hidden = fc_weight.shape[1]
    heads_here, head_part = qv_bias.shape[1:]
    head_dim = head_part * nd
    half = block // 2
    own_rows = rows // nt
    widths = (3 * local, local, hidden, hidden)
    vmem = pltpu.VMEM
    scratch = (
        [vmem((width, w), BF16) for w in widths]
        + [
            vmem((nd, 8, width), F32),
            vmem((8, width), F32),
            vmem((rows, 2 * rows), F32),
            vmem((rows, width), BF16),
            vmem((rows, local), BF16),
            vmem((2 * rows, 2 * local), BF16),
            vmem((heads_here, rows, 2 * rows), F32),
            vmem((rows, local), BF16),
            vmem((4, rows, width), BF16),
            vmem((4, nt - 1, own_rows, width), BF16),
            vmem((4, rows, width), BF16),
            vmem((own_rows, width), F32),
            vmem((rows, hidden), F32),
            vmem((rows, hidden), BF16),
            vmem((rows, hidden), BF16),
            vmem((own_rows, width), F32),
            vmem((rows, 2 * local), F32),
            vmem((rows, 2 * local), F32),
            vmem((rows, 2 * local), F32),
            vmem((rows, 3 * local), BF16),
        ]
        + [vmem((nd, 2, half, w), BF16) for w in widths]
        + [vmem((nd, half, w), BF16) for w in widths]
        + [vmem((nd, half, w), BF16) for w in widths]
        + [vmem((nd - 1, half, w), BF16) for w in widths]
        + [
            vmem((nt, 8, width), F32),
            vmem((8, width), F32),
            vmem((2, 8, width), F32),
            vmem((nd, 8, width), F32),
            pltpu.SemaphoreType.DMA((14 * (nd - 1) + 10 * (nt - 1) + 16,)),
            pltpu.SemaphoreType.DMA((14 * (nd - 1) + 10 * (nt - 1) + 16,)),
        ]
    )
    whole = pl.BlockSpec(memory_space=pltpu.VMEM)
    out_shapes = [
        (rows, width), (rows, width), (block, 3 * local), (block, local), (block, hidden),
        (block, hidden), norm_gains.shape, shifts.shape, fc_bias.shape, qv_bias.shape,
    ]
    results = pl.pallas_call(
        functools.partial(layer_kernel, nd, nt, head_dim),
        out_shape=[jax.ShapeDtypeStruct(shape, F32) for shape in out_shapes],
        in_specs=[whole] * 11,
        out_specs=[whole] * 10,
        scratch_shapes=scratch,
        compiler_params=pltpu.CompilerParams(
            collective_id=0, has_side_effects=True, vmem_limit_bytes=60 * 1024 * 1024
        ),
    )(
        block_input, out_grad, norm_gains, shifts, fc_bias, qv_bias, segment_ids,
        qkv_weight.reshape(block, 3 * local), proj_weight, fc_weight, out_weight,
    )
    g_qkv = results[2].reshape(block, 3, local)
    plain = results[:2] + results[3:]
    anywhere = pl.BlockSpec(memory_space=pl.ANY)
    output, input_grad, g_proj, g_fc, g_out, g_gains, g_shifts, g_fc_bias, g_qv = pl.pallas_call(
        functools.partial(move_kernel, len(plain)),
        out_shape=[jax.ShapeDtypeStruct(array.shape, F32) for array in plain],
        in_specs=[anywhere] * len(plain),
        out_specs=[anywhere] * len(plain),
        scratch_shapes=[pltpu.SemaphoreType.DMA((len(plain),))],
    )(*plain)
    return (output, input_grad, g_qkv, g_qv, g_proj, g_fc, g_fc_bias, g_out, g_gains, g_shifts)


def solution(mesh):
    in_specs = (
        P(("dp", "ctx"), None),
        P("dp", None, "tp"),
        P(None, "tp", "dp"),
        P("dp", "tp"),
        P("dp", "tp"),
        P("tp", "dp"),
        P("dp", "tp"),
        P(None, "dp"),
        P(None, "dp"),
        P("dp", None),
        P(("dp", "ctx"), None),
    )
    out_specs = (
        P(("dp", "ctx"), None),
        P(("dp", "ctx"), None),
        P("dp", None, "tp"),
        P(None, "tp", "dp"),
        P("dp", "tp"),
        P("dp", "tp"),
        P("tp", "dp"),
        P("dp", "tp"),
        P(None, "dp"),
        P(None, "dp"),
    )
    return jax.shard_map(
        functools.partial(per_device, mesh.shape["dp"], mesh.shape["tp"]),
        mesh=mesh, in_specs=in_specs, out_specs=out_specs, check_vma=False,
    )
```

```python
import functools

import jax
import jax.numpy as jnp
from jax import lax
from jax.experimental import pallas as pl
from jax.experimental.pallas import tpu as pltpu
from jax.sharding import PartitionSpec as P

EPSILON = 1e-05
MASKED_SCORE = -1e30
GELU_SCALE = 0.7978845608028654
F32, BF16 = jnp.float32, jnp.bfloat16
MESH = pl.DeviceIdType.MESH
TILE = 256


def normalize(values):
    centered = values - jnp.mean(values, axis=-1, keepdims=True)
    inverse = lax.rsqrt(jnp.mean(centered * centered, axis=-1, keepdims=True) + EPSILON)
    return centered * inverse, inverse


def norm_back(upstream, normed, inverse, gain_row):
    scaled = upstream * gain_row
    return inverse * (
        scaled
        - jnp.mean(scaled, axis=-1, keepdims=True)
        - normed * jnp.mean(scaled * normed, axis=-1, keepdims=True)
    )


def gelu_slope(pre_act):
    inner_arg = GELU_SCALE * (pre_act + 0.044715 * pre_act * pre_act * pre_act)
    tanh_val = jnp.tanh(inner_arg)
    activated = 0.5 * pre_act * (1.0 + tanh_val)
    slopes = 0.5 * (1.0 + tanh_val) + 0.5 * pre_act * (1.0 - tanh_val * tanh_val) * GELU_SCALE * (
        1.0 + 3.0 * 0.044715 * pre_act * pre_act
    )
    return (activated, slopes)


def dot_nn(a, b):
    return lax.dot_general(a, b, (((1,), (0,)), ((), ())), preferred_element_type=F32)


def dot_nt(a, b):
    return lax.dot_general(a, b, (((1,), (1,)), ((), ())), preferred_element_type=F32)


def dot_tn(a, b):
    return lax.dot_general(a, b, (((0,), (0,)), ((), ())), preferred_element_type=F32)


def loop(count, body):
    def step(j, carry):
        body(j)
        return carry

    lax.fori_loop(0, count, step, 0)


def tile_at(j, size=TILE):
    return pl.ds(pl.multiple_of(j * size, size), size)


def layer_kernel(
    nd, nt, head_dim,
    x_ref, gy_ref, gains_ref, shifts_ref, fcb_ref, qvb_ref, seg_ref, lq_ref, lp_ref, lf_ref, lo_ref,
    out_ref, ing_ref, gq_ref, gp_ref, gf_ref, go_ref, ggains_ref, gshifts_ref, gfcb_ref, gqvb_ref,
    wq, wp, wf, wo, small_in, small_f, mask_ref, ln1_s, q_s, kv_s, prob_s, attn_s,
    part, rs_in, ag, resid_s, dact_s, act_s, dpre_s, dresid_s, dkv_own, dkv_out, dkv_in, st_s,
    loc_q, loc_p, loc_f, loc_o, par_q, par_p, par_f, par_o,
    sum_q, sum_p, sum_f, sum_o, rcv_q, rcv_p, rcv_f, rcv_o,
    tp_small, own_small, ctx_small, dp_small, send_sems, recv_sems,
):
    d, c, t = lax.axis_index("dp"), lax.axis_index("ctx"), lax.axis_index("tp")
    other = 1 - c
    rows, width = x_ref.shape
    local = q_s.shape[1]
    hidden = act_s.shape[1]
    heads = local // head_dim
    block = lq_ref.shape[0]
    half = block // 2
    own_rows = rows // nt
    scale = head_dim ** (-0.5)
    count = [0]
    pending = []

    def send(src, dst, **where):
        i = count[0]
        count[0] += 1
        copy = pltpu.make_async_remote_copy(
            src_ref=src, dst_ref=dst, send_sem=send_sems.at[i], recv_sem=recv_sems.at[i],
            device_id=where, device_id_type=MESH,
        )
        copy.start()
        pending.append(copy)
        return copy

    def dp_at(k):
        return lax.rem(d + k, nd)

    def tp_at(k):
        return lax.rem(t + k, nt)

    def mine(size=own_rows):
        return pl.ds(pl.multiple_of(t * size, size), size)

    barrier = pltpu.get_barrier_semaphore()
    for k in range(1, nd):
        pl.semaphore_signal(barrier, inc=1, device_id={"dp": dp_at(k)}, device_id_type=MESH)
    for k in range(1, nt):
        pl.semaphore_signal(barrier, inc=1, device_id={"tp": tp_at(k)}, device_id_type=MESH)
    pl.semaphore_signal(barrier, inc=1, device_id={"ctx": other}, device_id_type=MESH)
    pl.semaphore_wait(barrier, nd + nt - 1)

    def place(shard):
        size = shard.shape[1]
        lanes = lax.broadcasted_iota(jnp.int32, (shard.shape[0], size * nd), 1)
        spread = jnp.concatenate([shard.astype(F32)] * nd, axis=1)
        return jnp.where((lanes >= d * size) & (lanes < (d + 1) * size), spread, 0.0)

    def in_a_row(tables):
        return jnp.concatenate([tab[r : r + 1] for tab in tables for r in range(tab.shape[0])], axis=1)


    def half_at(owner, core):
        return pl.ds(pl.multiple_of(owner * block + core * half, half), half)

    def gather(shard, whole):
        return [
            send(shard.at[pl.ds(pl.multiple_of(c * half, half), half)], whole.at[half_at(d, c)],
                 dp=dp_at(k))
            for k in range(1, nd)
        ]

    def hand_on(whole, copies):
        handed = []
        for k in range(1, nd):
            copies[k - 1].wait_recv()
            place = whole.at[half_at(lax.rem(d - k + nd, nd), c)]
            handed.append(send(place, place, ctx=other))
        return handed

    def arrive(copies):
        for copy in copies:
            copy.wait_recv()

    small_in[d, 0:2, :] = place(gains_ref[...])
    small_in[d, 2:6, :] = place(shifts_ref[...])
    small_in[d, 6:7, :] = in_a_row([place(fcb_ref[...])])
    small_in[d, 7:8, :] = jnp.zeros((1, width), F32)
    small_in[d, 7:8, 0 : 2 * local] = in_a_row([place(qvb_ref[m]) for m in range(2)])
    small_copies = [send(small_in.at[d], small_in.at[d], dp=dp_at(k)) for k in range(1, nd)]
    got_q = gather(lq_ref, wq)
    got_p = gather(lp_ref, wp)
    got_f = gather(lf_ref, wf)
    got_o = gather(lo_ref, wo)
    seg_own = seg_ref[:, pl.ds(pl.multiple_of(c * rows, rows), rows)].astype(F32)
    seg_rest = seg_ref[:, pl.ds(pl.multiple_of(other * rows, rows), rows)].astype(F32)
    seg_column = jnp.transpose(jnp.broadcast_to(seg_own, (128, rows)))[:, 0:1]
    seg_keys = jnp.concatenate([seg_own, seg_rest], axis=1)
    q_pos = c * rows + lax.broadcasted_iota(jnp.int32, (rows, 2 * rows), 0)
    lane = lax.broadcasted_iota(jnp.int32, (rows, 2 * rows), 1)
    k_pos = lane + jnp.where(lane < rows, c * rows, other * rows - rows)
    mask_ref[...] = jnp.where((seg_column == seg_keys) & (k_pos <= q_pos), 0.0, MASKED_SCORE)
    own_block = pl.ds(pl.multiple_of(d * block, block), block)
    for shard, whole in ((lq_ref, wq), (lp_ref, wp), (lf_ref, wf), (lo_ref, wo)):
        whole[own_block, :] = shard[...]
    arrive(small_copies)
    total = small_in[0]
    for k in range(1, nd):
        total = total + small_in[k]
    small_f[...] = total

    def first_norm(j):
        at = tile_at(j, own_rows)
        normed, _ = normalize(x_ref[at, :].astype(F32))
        ln1_s[at, :] = (normed * small_f[0:1, :] + small_f[2:3, :]).astype(BF16)

    loop(nt, first_norm)
    handed = hand_on(wq, got_q)
    arrive(handed)
    kv_s[0:rows, 0:local] = dot_nn(ln1_s[...], wq[:, local : 2 * local]).astype(BF16)
    kv_s[0:rows, local : 2 * local] = (
        dot_nn(ln1_s[...], wq[:, 2 * local : 3 * local]) + small_f[7:8, local : 2 * local]
    ).astype(BF16)
    kv_copy = send(kv_s.at[pl.ds(0, rows)], kv_s.at[pl.ds(rows, rows)], ctx=other)
    q_s[...] = (dot_nn(ln1_s[...], wq[:, 0:local]) + small_f[7:8, 0:local]).astype(BF16)
    handed_p = hand_on(wp, got_p)
    kv_copy.wait_recv()

    mixed = []
    for h in range(heads):
        at = slice(h * head_dim, (h + 1) * head_dim)
        vat = slice(local + h * head_dim, local + (h + 1) * head_dim)
        scores = dot_nt(q_s[:, at], kv_s[:, at]) * scale + mask_ref[...]
        top = jnp.max(scores, axis=-1, keepdims=True)
        log_total = top + jnp.log(jnp.sum(jnp.exp(scores - top), axis=-1, keepdims=True))
        probs = jnp.exp(scores - log_total)
        prob_s[h] = probs
        mixed.append(dot_nn(probs.astype(BF16), kv_s[:, vat]))
    attn_s[...] = jnp.concatenate(mixed, axis=1).astype(BF16)

    def reduce_start(i):
        return [
            send(part.at[i, pl.ds(pl.multiple_of(tp_at(k) * own_rows, own_rows), own_rows)],
                 rs_in.at[i, k - 1], tp=tp_at(k))
            for k in range(1, nt)
        ]

    def reduce_end(i, copies):
        total = part[i, mine(), :].astype(F32)
        for k in range(1, nt):
            copies[k - 1].wait_recv()
            total = total + rs_in[i, k - 1].astype(F32)
        return total

    def share(i, value):
        ag[i, mine(), :] = value.astype(BF16)
        place = ag.at[i, mine()]
        return [send(place, place, tp=tp_at(k)) for k in range(1, nt)]

    arrive(handed_p)

    def proj_tile(j):
        part[0, :, tile_at(j)] = dot_nt(attn_s[...], wp[tile_at(j), :]).astype(BF16)

    loop(width // TILE, proj_tile)
    reduced = reduce_start(0)
    handed_f = hand_on(wf, got_f)
    own_x = x_ref[mine(), :].astype(F32)
    resid = own_x + reduce_end(0, reduced) + small_f[4:5, :]
    resid_s[...] = resid
    normed2, _ = normalize(resid)
    shared = share(0, normed2 * small_f[1:2, :] + small_f[3:4, :])
    handed_o = hand_on(wo, got_o)
    arrive(handed_f)
    arrive(handed_o)

    def dact_tile(j):
        dact_s[:, tile_at(j)] = dot_nn(gy_ref[...], wo[:, tile_at(j)])

    loop(hidden // TILE, dact_tile)
    arrive(shared)

    def hidden_tile(j):
        at = tile_at(j)
        pre = dot_nn(ag[0], wf[:, at]) + small_f[6:7, at]
        activated, slopes = gelu_slope(pre)
        act_s[:, at] = activated.astype(BF16)
        dpre = (dact_s[:, at] * slopes).astype(BF16)
        dpre_s[:, at] = dpre
        own_small[6:7, at] = jnp.sum(dpre.astype(F32), axis=0, keepdims=True)

    loop(hidden // TILE, hidden_tile)

    def dln2_tile(j):
        part[1, :, tile_at(j)] = dot_nt(dpre_s[...], wf[tile_at(j), :]).astype(BF16)

    loop(width // TILE, dln2_tile)
    reduced1 = reduce_start(1)

    def down_tile(j):
        part[2, :, tile_at(j)] = dot_nt(act_s[...], wo[tile_at(j), :]).astype(BF16)

    loop(width // TILE, down_tile)

    tile_rows = max(TILE, block)
    blocks_in = tile_rows // block

    def grad_start(left, right, grads, partner):
        def tile(j):
            value = dot_tn(left[:, tile_at(j, tile_rows)], right[...]).astype(BF16)
            grads[pl.ds(j * blocks_in, blocks_in)] = value.reshape(
                (blocks_in, 2, half, value.shape[1])
            )

        loop(width // tile_rows, tile)
        return send(grads.at[:, other], partner, ctx=other)

    def grad_spread(copy, grads, partner, sums, received):
        copy.wait_recv()

        def add(j):
            sums[j] = (grads[j, c].astype(F32) + partner[j].astype(F32)).astype(BF16)

        loop(nd, add)
        return [send(sums.at[dp_at(k)], received.at[k - 1], dp=dp_at(k)) for k in range(1, nd)]

    def grad_end(copies, sums, received, result):
        total = sums[d].astype(F32)
        for k in range(1, nd):
            copies[k - 1].wait_recv()
            total = total + received[k - 1].astype(F32)
        place = pl.ds(pl.multiple_of(c * half, half), half)
        result[place, :] = total
        return send(result.at[place], result.at[place], ctx=other)

    pair_o = grad_start(gy_ref, act_s, loc_o, par_o)

    dln2 = reduce_end(1, reduced1)
    normed2, inverse2 = normalize(resid_s[...])
    own_gy = gy_ref[mine(), :].astype(F32)
    dresid = own_gy + norm_back(dln2, normed2, inverse2, small_f[1:2, :])
    shared1 = share(1, dresid)
    reduced2 = reduce_start(2)
    dresid_s[...] = dresid
    tp_small[t, 1:2, :] = jnp.sum(dln2 * normed2, axis=0, keepdims=True)
    tp_small[t, 3:4, :] = jnp.sum(dln2, axis=0, keepdims=True)
    tp_small[t, 4:5, :] = jnp.sum(dresid, axis=0, keepdims=True)
    tp_small[t, 5:6, :] = jnp.sum(own_gy, axis=0, keepdims=True)
    spread_o = grad_spread(pair_o, loc_o, par_o, sum_o, rcv_o)
    pair_f = grad_start(ag.at[0], dpre_s, loc_f, par_f)
    arrive(shared1)

    dattn = dot_nn(ag[1], wp[...]).astype(BF16)
    dq_parts, dk_parts, dv_parts = [], [], []
    for h in range(heads):
        at = slice(h * head_dim, (h + 1) * head_dim)
        vat = slice(local + h * head_dim, local + (h + 1) * head_dim)
        dattn_h = dattn[:, at]
        probs = prob_s[h]
        delta = jnp.sum(
            dattn_h.astype(F32) * attn_s[:, at].astype(F32), axis=-1, keepdims=True
        )
        dprob = dot_nt(dattn_h, kv_s[:, vat])
        dscore = (probs * (dprob - delta) * scale).astype(BF16)
        dq_parts.append(dot_nn(dscore, kv_s[:, at]))
        dk_parts.append(dot_tn(dscore, q_s[:, at]))
        dv_parts.append(dot_tn(probs.astype(BF16), dattn_h))
    dkv = jnp.concatenate(dk_parts + dv_parts, axis=1)
    dkv_out[...] = dkv[rows:, :]
    dkv_copy = send(dkv_out, dkv_in, ctx=other)
    dkv_own[...] = dkv[:rows, :]
    dq = jnp.concatenate(dq_parts, axis=1).astype(BF16)
    st_s[:, 0:local] = dq
    spread_f = grad_spread(pair_f, loc_f, par_f, sum_f, rcv_f)
    dkv_copy.wait_recv()
    st_s[:, local : 3 * local] = (dkv_own[...] + dkv_in[...]).astype(BF16)

    def dln1_tile(j):
        part[3, :, tile_at(j)] = dot_nt(st_s[...], wq[tile_at(j), :]).astype(BF16)

    loop(width // TILE, dln1_tile)
    reduced3 = reduce_start(3)
    pair_q = grad_start(ln1_s, st_s, loc_q, par_q)
    pair_p = grad_start(ag.at[1], attn_s, loc_p, par_p)
    own_small[7:8, :] = jnp.zeros((1, width), F32)
    own_small[7:8, 0:local] = jnp.sum(st_s[:, 0:local].astype(F32), axis=0, keepdims=True)
    own_small[7:8, local : 2 * local] = jnp.sum(
        st_s[:, 2 * local : 3 * local].astype(F32), axis=0, keepdims=True
    )
    spread_q = grad_spread(pair_q, loc_q, par_q, sum_q, rcv_q)
    spread_p = grad_spread(pair_p, loc_p, par_p, sum_p, rcv_p)

    shared2 = share(2, resid_s[...] + reduce_end(2, reduced2) + small_f[5:6, :])
    dln1 = reduce_end(3, reduced3)
    normed1, inverse1 = normalize(x_ref[mine(), :].astype(F32))
    shared3 = share(3, dresid_s[...] + norm_back(dln1, normed1, inverse1, small_f[0:1, :]))
    tp_small[t, 0:1, :] = jnp.sum(dln1 * normed1, axis=0, keepdims=True)
    tp_small[t, 2:3, :] = jnp.sum(dln1, axis=0, keepdims=True)
    tp_small[t, 6:8, :] = jnp.zeros((2, width), F32)
    small_tp = [send(tp_small.at[t], tp_small.at[t], tp=tp_at(k)) for k in range(1, nt)]
    end_o = grad_end(spread_o, sum_o, rcv_o, go_ref)
    end_f = grad_end(spread_f, sum_f, rcv_f, gf_ref)
    arrive(small_tp)
    total = tp_small[0]
    for k in range(1, nt):
        total = total + tp_small[k]
    ctx_small[c, 0:6, :] = total[0:6]
    ctx_small[c, 6:8, :] = own_small[6:8, :]
    small_ctx = send(ctx_small.at[c], ctx_small.at[c], ctx=other)
    arrive(shared2)
    out_ref[...] = ag[2].astype(F32)
    small_ctx.wait_recv()
    dp_small[d] = ctx_small[0] + ctx_small[1]
    small_dp = [send(dp_small.at[d], dp_small.at[d], dp=dp_at(k)) for k in range(1, nd)]
    end_q = grad_end(spread_q, sum_q, rcv_q, gq_ref)
    end_p = grad_end(spread_p, sum_p, rcv_p, gp_ref)
    arrive(small_dp)
    total = dp_small[0]
    for k in range(1, nd):
        total = total + dp_small[k]

    def own_part(table):
        size = table.shape[1] // nd
        part_here = jnp.zeros((table.shape[0], size), F32)
        for k in range(nd):
            part_here = jnp.where(d == k, table[:, k * size : (k + 1) * size], part_here)
        return part_here

    def as_table(row, columns, count):
        return jnp.concatenate(
            [row[:, r * columns : (r + 1) * columns] for r in range(count)], axis=0
        )

    ggains_ref[...] = own_part(total[0:2])
    gshifts_ref[...] = own_part(total[2:6])
    table_rows = fcb_ref.shape[0]
    gfcb_ref[...] = own_part(as_table(total[6:7], hidden // table_rows, table_rows))
    for m in range(2):
        gqvb_ref[m] = own_part(as_table(total[7:8, m * local : (m + 1) * local], head_dim, heads))
    arrive(shared3)
    ing_ref[...] = ag[3].astype(F32)
    arrive([end_o, end_f, end_q, end_p])
    for copy in pending:
        copy.wait_send()


def per_device(
    nd, nt,
    block_input, qkv_weight, qv_bias, proj_weight, fc_weight, fc_bias, out_weight,
    norm_gains, shifts, segment_ids, out_grad,
):
    rows, width = block_input.shape
    block, _, local = qkv_weight.shape
    hidden = fc_weight.shape[1]
    heads_here, head_part = qv_bias.shape[1:]
    head_dim = head_part * nd
    half = block // 2
    own_rows = rows // nt
    widths = (3 * local, local, hidden, hidden)
    vmem = pltpu.VMEM
    scratch = (
        [vmem((width, w), BF16) for w in widths]
        + [
            vmem((nd, 8, width), F32),
            vmem((8, width), F32),
            vmem((rows, 2 * rows), F32),
            vmem((rows, width), BF16),
            vmem((rows, local), BF16),
            vmem((2 * rows, 2 * local), BF16),
            vmem((heads_here, rows, 2 * rows), F32),
            vmem((rows, local), BF16),
            vmem((4, rows, width), BF16),
            vmem((4, nt - 1, own_rows, width), BF16),
            vmem((4, rows, width), BF16),
            vmem((own_rows, width), F32),
            vmem((rows, hidden), F32),
            vmem((rows, hidden), BF16),
            vmem((rows, hidden), BF16),
            vmem((own_rows, width), F32),
            vmem((rows, 2 * local), F32),
            vmem((rows, 2 * local), F32),
            vmem((rows, 2 * local), F32),
            vmem((rows, 3 * local), BF16),
        ]
        + [vmem((nd, 2, half, w), BF16) for w in widths]
        + [vmem((nd, half, w), BF16) for w in widths]
        + [vmem((nd, half, w), BF16) for w in widths]
        + [vmem((nd - 1, half, w), BF16) for w in widths]
        + [
            vmem((nt, 8, width), F32),
            vmem((8, width), F32),
            vmem((2, 8, width), F32),
            vmem((nd, 8, width), F32),
            pltpu.SemaphoreType.DMA((14 * (nd - 1) + 10 * (nt - 1) + 16,)),
            pltpu.SemaphoreType.DMA((14 * (nd - 1) + 10 * (nt - 1) + 16,)),
        ]
    )
    whole = pl.BlockSpec(memory_space=pltpu.VMEM)
    out_shapes = [
        (rows, width), (rows, width), (block, 3 * local), (block, local), (block, hidden),
        (block, hidden), norm_gains.shape, shifts.shape, fc_bias.shape, qv_bias.shape,
    ]
    results = pl.pallas_call(
        functools.partial(layer_kernel, nd, nt, head_dim),
        out_shape=[jax.ShapeDtypeStruct(shape, F32) for shape in out_shapes],
        in_specs=[whole] * 11,
        out_specs=[whole] * 10,
        scratch_shapes=scratch,
        compiler_params=pltpu.CompilerParams(
            collective_id=0, has_side_effects=True, vmem_limit_bytes=60 * 1024 * 1024
        ),
    )(
        block_input, out_grad, norm_gains, shifts, fc_bias, qv_bias, segment_ids,
        qkv_weight.reshape(block, 3 * local), proj_weight, fc_weight, out_weight,
    )
    g_qkv = results[2].reshape(block, 3, local)
    output, input_grad, _, g_proj, g_fc, g_out, g_gains, g_shifts, g_fc_bias, g_qv = results
    return (output, input_grad, g_qkv, g_qv, g_proj, g_fc, g_fc_bias, g_out, g_gains, g_shifts)


def solution(mesh):
    in_specs = (
        P(("dp", "ctx"), None),
        P("dp", None, "tp"),
        P(None, "tp", "dp"),
        P("dp", "tp"),
        P("dp", "tp"),
        P("tp", "dp"),
        P("dp", "tp"),
        P(None, "dp"),
        P(None, "dp"),
        P("dp", None),
        P(("dp", "ctx"), None),
    )
    out_specs = (
        P(("dp", "ctx"), None),
        P(("dp", "ctx"), None),
        P("dp", None, "tp"),
        P(None, "tp", "dp"),
        P("dp", "tp"),
        P("dp", "tp"),
        P("tp", "dp"),
        P("dp", "tp"),
        P(None, "dp"),
        P(None, "dp"),
    )
    return jax.shard_map(
        functools.partial(per_device, mesh.shape["dp"], mesh.shape["tp"]),
        mesh=mesh, in_specs=in_specs, out_specs=out_specs, check_vma=False,
    )
```
